1024 devices in a mesh: dp: 8 (over y), fsdp: 16 (over z, core), tensor: 8 (over x).
Axes of the slice: x: 8, y: 8, z: 8, core: 2. Of those that a mesh axis runs over, the one named last changes fastest.
Arguments:
- momentum: float32 [8192, 28672], P('fsdp', 'tensor'), may hold values from -180 to 180, as said below
- previous: bfloat16 [28672, 128], P('tensor'), may hold values from -6 to 6
Outputs:
- left_factor: float32 [8192, 128], P('fsdp')
- right_factor: bfloat16 [28672, 128], P('tensor')
- column_scale: float32 [128], replicated
The draws below stay inside these ranges and needn't reach their ends.
Inputs may be any that keep to these rules, and one draw needn't show every extreme that they name: momentum entries are finite.
All inputs are finite; a program needn't handle non-finite values.
Results may differ from the reference program's by a relative error of at most 0.00055.
Values may be sent and summed in bfloat16 or wider, within the bound.
A program may use at most 32 MiB of HBM per device.

```python
import math
import jax
import jax.numpy as jnp
from jax import lax

NR = 8192
NC = 28672
RANK = 128


def draw_momentum(key, part):
    key = jax.random.fold_in(key, 11)
    key_base, key_row, key_col = jax.random.split(key, 3)
    base = jnp.clip(jax.random.normal(key_base, (NR, NC), jnp.float32), -6.0, 6.0)
    spread = 10.0
    row_scale = jnp.exp(jax.random.uniform(key_row, (NR, 1), jnp.float32) * jnp.log(spread))
    ramp = 1.0 + 2.0 * jnp.arange(NC, dtype=jnp.float32) / NC
    col_scale = jnp.exp(jax.random.uniform(key_col, (1, NC), jnp.float32) * jnp.log(spread)) * ramp[None, :]
    return 0.1 * base * row_scale * col_scale


def block_scale(rng, shape, pieces, smallest, largest):
    def one(axis_at, parts):
        heights = jax.random.uniform(jax.random.fold_in(jax.random.fold_in(rng, 6), axis_at), (parts,), jnp.float32, smallest / len(pieces), largest / len(pieces))
        return jnp.repeat(jnp.exp(heights), shape[axis_at] // parts).reshape((-1,) + (1,) * (len(shape) - axis_at - 1))

    level = one(*pieces[0])
    for cut in pieces[1:]:
        level = level * one(*cut)
    return level


def noise(rng, dims, width, limit, pieces=(), kind=jnp.bfloat16):
    array = width * jax.random.normal(rng, dims, jnp.float32)
    if pieces:
        array = array * block_scale(rng, dims, pieces, -0.22, 0.18)
    return jnp.clip(array, -limit, limit).astype(kind)


def setup_inputs(seed: int = 0) -> dict:
    key_of = jax.random.split(jax.random.key(seed), 3)
    return {
        "momentum": draw_momentum(jax.random.fold_in(key_of[2], 71), 0),
        "previous": noise(key_of[1], (NC, RANK), 1.0, 6.0, ((0, 8),)),
    }


def whiten(matrix, lower_factor):
    return lax.linalg.triangular_solve(lower_factor, matrix, left_side=False, lower=True, transpose_a=True)

def reference(momentum, previous):
    power = jnp.dot(momentum, previous.astype(jnp.float32), precision=lax.Precision.HIGHEST)
    gram = jnp.dot(power.T, power, precision=lax.Precision.HIGHEST)
    lower_factor = jnp.linalg.cholesky(gram)
    ortho = whiten(power, lower_factor)
    feedback = jnp.dot(momentum.T, ortho, precision=lax.Precision.HIGHEST)
    column = jnp.sqrt(lax.optimization_barrier(jnp.sum(feedback * feedback, axis=0)) + 1e-06)
    left_factor = ortho * math.sqrt(NR)
    right_factor = (feedback * (math.sqrt(NC) / column)).astype(jnp.bfloat16)
    return (left_factor, right_factor, column / math.sqrt(NC))
```

```python
import functools
import math

import jax
import jax.numpy as jnp
from jax import lax
from jax.experimental import pallas as pl
from jax.experimental.pallas import tpu as pltpu
from jax.sharding import PartitionSpec as P

HIGHEST = lax.Precision.HIGHEST
MESH = pl.DeviceIdType.MESH
RANK = 128
F32 = jnp.float32


def aligned(value, multiple=8):
    return pl.multiple_of(value, multiple)


def invert_cholesky(a_ref, linv_ref):
    shape = (8, RANK)
    sub = lax.broadcasted_iota(jnp.int32, shape, 0)
    lane = lax.broadcasted_iota(jnp.int32, shape, 1)

    def row_of(v, p):
        return jnp.broadcast_to(v[p : p + 1, :], shape)

    def block(k, carry):
        off = aligned(k * 8)
        rows = a_ref[pl.ds(off, 8), :]
        turned = pltpu.roll(rows, lax.rem(RANK - off, RANK), 1)
        cols = [jnp.broadcast_to(turned[:, q : q + 1], shape) for q in range(8)]
        rel = lane - off
        scale = jnp.zeros(shape, F32)
        for p in range(8):
            pivot = row_of(cols[p], p)
            factor = jnp.where(sub > p, cols[p] * (1.0 / pivot), 0.0)
            pivot_row = row_of(rows, p)
            for q in range(p + 1, 8):
                cols[q] = cols[q] - factor * row_of(cols[q], p)
            rows = jnp.where((rel == p) & (sub > p), 0.0, rows) - factor * jnp.where(rel == p, 1.0, pivot_row)
            scale = jnp.where(sub == p, lax.rsqrt(pivot), scale)
        panel = jnp.where(rel == sub, 1.0, rows) * scale
        panel = jnp.where((rel > sub) & (rel < 8), 0.0, panel)
        linv_ref[pl.ds(off, 8), :] = jnp.where(rel <= sub, panel, 0.0)
        upper = jnp.where(rel >= 8, panel, 0.0)
        update = lax.dot_general(
            upper, panel, (((0,), (0,)), ((), ())), precision=HIGHEST, preferred_element_type=F32
        )
        row = lax.broadcasted_iota(jnp.int32, (RANK, RANK), 0)
        col = lax.broadcasted_iota(jnp.int32, (RANK, RANK), 1) - off
        a = a_ref[...]
        a_ref[...] = jnp.where(
            row >= off + 8, jnp.where((col >= 0) & (col < 8), 0.0, a) - update, a
        )
        return carry

    lax.fori_loop(0, RANK // 8, block, 0)


def body(
    sizes, m_ref, p_ref, left_ref, right_ref, column_ref,
    p_v, mrow, mcol, wpart, rsw, wfull, gpart, rsg, gfull, work, linv, zpart, rsz, zfull, nsend, nrecv, nrow, nplane,
    load_sem, send_sem, recv_sem,
):
    dn, fn, tn, nr, nc = sizes
    zn = fn // 2
    mr, mc = m_ref.shape
    wr = mr // dn
    br = wr // tn
    cy = mc // dn
    cz = cy // zn
    cores = ((0, (cz // 16 + 1) * 8), ((cz // 16 + 1) * 8, cz - (cz // 16 + 1) * 8))
    gr = RANK // fn
    width = mcol.shape[1]
    y, f, x = lax.axis_index("dp"), lax.axis_index("fsdp"), lax.axis_index("tensor")
    z, c = f // 2, lax.rem(f, 2)

    def at(dy=0, df=0, dx=0):
        return (lax.rem(y + dy, dn), lax.rem(f + df, fn), lax.rem(x + dx, tn))

    def send(src, dst, phase, device):
        pltpu.make_async_remote_copy(
            src_ref=src, dst_ref=dst, send_sem=send_sem.at[phase], recv_sem=recv_sem.at[phase],
            device_id=device, device_id_type=MESH,
        ).start()

    def wait(ref, sem):
        pltpu.make_async_copy(ref, ref, sem).wait()

    def by_core(fun):
        for core, (start, length) in enumerate(cores):
            pl.when(c == core)(functools.partial(fun, start, length))

    lines_x = [at(dx=i) for i in range(1, tn)]
    lines_f = [at(df=i) for i in range(1, fn)]
    plane = [at(dy=i, dx=j) for i in range(dn) for j in range(tn) if i or j]

    barrier = pltpu.get_barrier_semaphore()
    for device in plane + lines_f:
        pl.semaphore_signal(barrier, inc=1, device_id=device, device_id_type=MESH)

    first_col = (cy * y) // 128 * 128
    skip = aligned(cy * y - first_col)
    load_p = pltpu.make_async_copy(p_ref, p_v, load_sem.at[0])
    load_row = pltpu.make_async_copy(m_ref.at[pl.ds(aligned(wr * y), wr)], mrow, load_sem.at[1])
    load_col = pltpu.make_async_copy(
        m_ref.at[:, pl.ds(aligned(first_col, 128), width)], mcol, load_sem.at[2]
    )
    load_p.start()
    load_row.start()
    load_col.start()
    load_p.wait()
    load_row.wait()

    step = 512 if mc % 512 == 0 else 128

    def power_step(i, total):
        at_k = aligned(i * step, 128)
        m = mrow[:, pl.ds(at_k, step)]
        first = m.astype(jnp.bfloat16)
        rest = m - first.astype(F32)
        second = rest.astype(jnp.bfloat16)
        third = (rest - second.astype(F32)).astype(jnp.bfloat16)
        terms = jnp.concatenate([first, second, third], axis=0)
        return total + jnp.dot(terms, p_v[pl.ds(at_k, step), :], preferred_element_type=F32)

    terms = lax.fori_loop(0, mc // step, power_step, jnp.zeros((3 * wr, RANK), F32))
    wpart[...] = terms[:wr] + (terms[wr : 2 * wr] + terms[2 * wr :])

    pl.semaphore_wait(barrier, len(plane) + len(lines_f))

    for i, device in enumerate(lines_x):
        to = lax.rem(x + 1 + i, tn)
        send(wpart.at[pl.ds(aligned(to * br), br)], rsw.at[x], 0, device)
    rsw[x] = wpart[pl.ds(aligned(x * br), br), :]
    wait(rsw.at[pl.ds(0, tn - 1)], recv_sem.at[0])
    mine = aligned((y * tn + x) * br)
    total = rsw[0]
    for i in range(1, tn):
        total = total + rsw[i]
    wfull[pl.ds(mine, br), :] = total

    for device in plane:
        send(wfull.at[pl.ds(mine, br)], wfull.at[pl.ds(mine, br)], 1, device)
    load_col.wait()
    wait(wfull.at[pl.ds(0, mr - br)], recv_sem.at[1])

    w = wfull[...]
    gpart[...] = lax.dot_general(w, w, (((0,), (0,)), ((), ())), precision=HIGHEST, preferred_element_type=F32)
    for i, device in enumerate(lines_f):
        to = lax.rem(f + 1 + i, fn)
        send(gpart.at[pl.ds(aligned(to * gr), gr)], rsg.at[f], 2, device)
    rsg[f] = gpart[pl.ds(aligned(f * gr), gr), :]

    zpart[...] = lax.dot_general(
        mcol[...], w, (((0,), (0,)), ((), ())), precision=HIGHEST, preferred_element_type=F32
    )
    for i in range(zn):
        to_z = lax.rem(z + i, zn)
        for core, (start, length) in enumerate(cores):

            def send_part(start=start, length=length, core=core):
                send(
                    zpart.at[pl.ds(aligned(skip + to_z * cz + start), length)],
                    rsz.at[f, pl.ds(0, length)], 3, (y, 2 * to_z + core, x),
                )

            if i:
                send_part()
            else:
                pl.when(c != core)(send_part)

    wait(rsg.at[pl.ds(0, fn - 1)], recv_sem.at[2])
    total = rsg[0]
    for i in range(1, fn):
        total = total + rsg[i]
    gmine = aligned(f * gr)
    gfull[pl.ds(gmine, gr), :] = total
    for device in lines_f:
        send(gfull.at[pl.ds(gmine, gr)], gfull.at[pl.ds(gmine, gr)], 4, device)

    block = y * zn + z

    def share(start, length):
        rsz[f, pl.ds(0, length)] = zpart[pl.ds(aligned(skip + z * cz + start), length), :]
        wait(rsz.at[pl.ds(0, fn - 1), pl.ds(0, length)], recv_sem.at[3])
        total = rsz[0, pl.ds(0, length)]
        for i in range(1, fn):
            total = total + rsz[i, pl.ds(0, length)]
        zfull[block, pl.ds(start, length)] = total
        own = zfull.at[block, pl.ds(start, length)]
        for i in range(1, dn):
            send(own, own, 5, at(dy=i))
        for i in range(1, zn):
            send(own, own, 5, at(df=2 * i))

    by_core(share)

    wait(gfull.at[pl.ds(0, RANK - gr)], recv_sem.at[4])
    work[...] = gfull[...]
    invert_cholesky(work, linv)

    def squares(start, length):
        fb = lax.dot_general(
            zfull[block, pl.ds(start, length)], linv[...], (((1,), (1,)), ((), ())),
            precision=HIGHEST, preferred_element_type=F32,
        )
        nsend[...] = jnp.sum((fb * fb).reshape(length // 8, 8, RANK), axis=0)

    by_core(squares)
    for device in lines_f:
        send(nsend, nrecv.at[f], 6, device)
    nrecv[f] = nsend[...]

    even = lax.rem(y + z, 2)

    def forward(start, length):
        wait(zfull.at[pl.ds(0, dn + zn - 2), pl.ds(0, length)], recv_sem.at[5])
        for o in range(1, dn):

            def along_z(o=o):
                ref = zfull.at[lax.rem(y + o, dn) * zn + z, pl.ds(start, length)]
                for i in range(1, zn):
                    send(ref, ref, 7, at(df=2 * i))

            pl.when(even == o % 2)(along_z)
        for o in range(1, zn):

            def along_y(o=o):
                ref = zfull.at[y * zn + lax.rem(z + o, zn), pl.ds(start, length)]
                for i in range(1, dn):
                    send(ref, ref, 7, at(dy=i))

            pl.when(even != o % 2)(along_y)

    by_core(forward)

    left_ref[...] = lax.dot_general(
        wfull[...], linv[...] * math.sqrt(nr), (((1,), (1,)), ((), ())), precision=HIGHEST,
        preferred_element_type=F32,
    )

    wait(nrecv.at[pl.ds(0, fn - 1)], recv_sem.at[6])
    total = nrecv[0]
    for i in range(1, fn):
        total = total + nrecv[i]
    nrow[...] = jnp.sum(total, axis=0, keepdims=True)
    for device in plane:
        send(nrow, nplane.at[y * tn + x], 8, device)
    nplane[y * tn + x] = nrow[...]

    def rows_here(start, length):
        wait(zfull.at[pl.ds(0, (dn - 1) * (zn - 1)), pl.ds(0, length)], recv_sem.at[7])
        half = zfull.at[:, pl.ds(start, length)]
        send(half, half, 9, (y, f + 1 - 2 * c, x))

    by_core(rows_here)

    wait(nplane.at[pl.ds(0, dn * tn - 1)], recv_sem.at[8])
    column = jnp.sqrt(jnp.sum(nplane[...], axis=0) + 1e-06)
    column_ref[...] = column / math.sqrt(nc)
    factor = jnp.transpose(linv[...]) * (math.sqrt(nc) / column)
    work[...] = factor

    def rows_there(start, length):
        other = cz - length
        wait(zfull.at[:, pl.ds(0, other)], recv_sem.at[9])

    by_core(rows_there)

    per = 2 if cz % 16 else 1

    def finish(i, carry):
        rows = zfull[pl.ds(i * per, per)].reshape(per * cz, RANK)
        out = jnp.dot(rows, work[...], precision=HIGHEST, preferred_element_type=F32)
        right_ref[pl.ds(aligned(i * per * cz, 16), per * cz), :] = out.astype(jnp.bfloat16)
        return carry

    lax.fori_loop(0, dn * zn // per, finish, 0)

    wait(rsw.at[pl.ds(0, tn - 1)], send_sem.at[0])
    wait(wfull.at[pl.ds(0, mr - br)], send_sem.at[1])
    wait(rsg.at[pl.ds(0, fn - 1)], send_sem.at[2])
    wait(gfull.at[pl.ds(0, RANK - gr)], send_sem.at[4])
    wait(nrecv.at[pl.ds(0, fn - 1)], send_sem.at[6])
    wait(nplane.at[pl.ds(0, dn * tn - 1)], send_sem.at[8])

    def drain(start, length):
        wait(zpart.at[pl.ds(0, cy - length)], send_sem.at[3])
        wait(zfull.at[pl.ds(0, dn + zn - 2), pl.ds(0, length)], send_sem.at[5])
        wait(zfull.at[pl.ds(0, (dn - 1) * (zn - 1)), pl.ds(0, length)], send_sem.at[7])
        wait(zfull.at[:, pl.ds(0, length)], send_sem.at[9])

    by_core(drain)


def shards(sizes, momentum, previous):
    dn, fn, tn, nr, nc = sizes
    mr, mc = momentum.shape
    wr = mr // dn
    br = wr // tn
    cy = mc // dn
    zn = fn // 2
    cz = cy // zn
    most = (cz // 16 + 1) * 8
    width = -(-cy // 128) * 128
    vmem = pltpu.VMEM
    left, right, column = pl.pallas_call(
        functools.partial(body, sizes),
        out_shape=(
            jax.ShapeDtypeStruct((mr, RANK), F32),
            jax.ShapeDtypeStruct((mc, RANK), jnp.bfloat16),
            jax.ShapeDtypeStruct((1, RANK), F32),
        ),
        in_specs=[pl.BlockSpec(memory_space=pl.ANY)] * 2,
        out_specs=(pl.BlockSpec(memory_space=vmem),) * 3,
        scratch_shapes=[
            vmem((mc, RANK), jnp.bfloat16),
            vmem((wr, mc), F32),
            vmem((mr, width), F32),
            vmem((wr, RANK), F32),
            vmem((tn, br, RANK), F32),
            vmem((mr, RANK), F32),
            vmem((RANK, RANK), F32),
            vmem((fn, RANK // fn, RANK), F32),
            vmem((RANK, RANK), F32),
            vmem((RANK, RANK), F32),
            vmem((RANK, RANK), F32),
            vmem((width, RANK), F32),
            vmem((fn, most, RANK), F32),
            vmem((dn * zn, cz, RANK), F32),
            vmem((8, RANK), F32),
            vmem((fn, 8, RANK), F32),
            vmem((1, RANK), F32),
            vmem((dn * tn, 1, RANK), F32),
            pltpu.SemaphoreType.DMA((3,)),
            pltpu.SemaphoreType.DMA((10,)),
            pltpu.SemaphoreType.DMA((10,)),
        ],
        compiler_params=pltpu.CompilerParams(
            collective_id=0, has_side_effects=True, vmem_limit_bytes=40 * 2**20
        ),
    )(momentum, previous)
    return left, right, column.reshape(RANK)


def solution(mesh):
    dn, fn, tn = (mesh.shape[name] for name in ("dp", "fsdp", "tensor"))

    def run(momentum, previous):
        sizes = (dn, fn, tn, momentum.shape[0], momentum.shape[1])
        return jax.shard_map(
            functools.partial(shards, sizes),
            mesh=mesh,
            in_specs=(P("fsdp", "tensor"), P("tensor", None)),
            out_specs=(P("fsdp", None), P("tensor", None), P()),
            check_vma=False,
        )(momentum, previous)

    return run
```

```python
import functools
import math

import jax
import jax.numpy as jnp
from jax import lax
from jax.experimental import pallas as pl
from jax.experimental.pallas import tpu as pltpu
from jax.sharding import PartitionSpec as P

HIGHEST = lax.Precision.HIGHEST
MESH = pl.DeviceIdType.MESH
LIMIT = 51 * 2**20
RANK = 128
F32 = jnp.float32


def aligned(value, multiple=8):
    return pl.multiple_of(value, multiple)


STEP = 16


def split(v):
    first = v.astype(jnp.bfloat16)
    rest = v - first.astype(F32)
    second = rest.astype(jnp.bfloat16)
    return first, second, (rest - second.astype(F32)).astype(jnp.bfloat16)


def dot(a, b, ca, cb, precision=None):
    return lax.dot_general(
        a, b, (((ca,), (cb,)), ((), ())), precision=precision, preferred_element_type=F32
    )


def invert_cholesky(a_ref, linv_ref, first, last):
    shape = (STEP, RANK)
    sub = lax.broadcasted_iota(jnp.int32, shape, 0)
    lane = lax.broadcasted_iota(jnp.int32, shape, 1)
    row = lax.broadcasted_iota(jnp.int32, (RANK, RANK), 0)
    col = lax.broadcasted_iota(jnp.int32, (RANK, RANK), 1)

    def row_of(v, p):
        return jnp.broadcast_to(v[p : p + 1, :], shape)

    def block(k, carry):
        off = aligned(k * STEP, STEP)
        rows = a_ref[pl.ds(off, STEP), :]
        turned = pltpu.roll(rows, lax.rem(RANK - off, RANK), 1)
        cols = [jnp.broadcast_to(turned[:, q : q + 1], shape) for q in range(STEP)]
        rel = lane - off
        scale = jnp.zeros(shape, F32)
        for p in range(STEP):
            pivot = row_of(cols[p], p)
            factor = jnp.where(sub > p, cols[p] * (1.0 / pivot), 0.0)
            pivot_row = row_of(rows, p)
            for q in range(p + 1, STEP):
                cols[q] = cols[q] - factor * row_of(cols[q], p)
            rows = jnp.where((rel == p) & (sub > p), 0.0, rows) - factor * jnp.where(rel == p, 1.0, pivot_row)
            scale = jnp.where(sub == p, lax.rsqrt(pivot), scale)
        panel = jnp.where(rel == sub, 1.0, rows) * scale
        panel = jnp.where((rel > sub) & (rel < STEP), 0.0, panel)
        linv_ref[pl.ds(off, STEP), :] = jnp.where(rel <= sub, panel, 0.0)
        upper = jnp.where(rel >= STEP, panel, 0.0)
        u1, u2, u3 = split(upper)
        p1, p2, p3 = split(panel)
        update = dot(
            jnp.concatenate([u1, u1, u1, u2, u2, u3], axis=0),
            jnp.concatenate([p1, p2, p3, p1, p2, p1], axis=0), 0, 0,
        )
        a = a_ref[...]
        inside = (col >= off) & (col < off + STEP)
        a_ref[...] = jnp.where(row >= off + STEP, jnp.where(inside, 0.0, a) - update, a)
        return carry

    lax.fori_loop(first, last, block, 0)


def body(
    sizes, m_ref, p_ref, left_ref, fb_ref, column_ref, scale_ref,
    p_v, mrow, mcol, wpart, rsw, wfull, gpart, rsg, gfull, work, linv, zpart, rsz, zfull, nsend, nrecv, ntotal, nline,
    load_sem, send_sem, recv_sem,
):
    dn, fn, tn, nr, nc = sizes
    zn = fn // 2
    mr, mc = m_ref.shape
    wr = mr // dn
    br = wr // tn
    cy = mc // dn
    cz = cy // zn
    cores = pieces_of(cz)
    gr = RANK // fn
    width = mcol.shape[1]
    y, f, x = lax.axis_index("dp"), lax.axis_index("fsdp"), lax.axis_index("tensor")
    z, c = f // 2, lax.rem(f, 2)

    def at(dy=0, df=0, dx=0):
        return (lax.rem(y + dy, dn), lax.rem(f + df, fn), lax.rem(x + dx, tn))

    def send(src, dst, phase, device):
        pltpu.make_async_remote_copy(
            src_ref=src, dst_ref=dst, send_sem=send_sem.at[phase], recv_sem=recv_sem.at[phase],
            device_id=device, device_id_type=MESH,
        ).start()

    def wait(ref, sem):
        pltpu.make_async_copy(ref, ref, sem).wait()

    def by_core(fun, *args):
        for core in range(2):
            pl.when(c == core)(functools.partial(fun, core, *args))

    lines_x = [at(dx=i) for i in range(1, tn)]
    lines_y = [at(dy=i) for i in range(1, dn)]
    lines_f = [at(df=i) for i in range(1, fn)]
    lines_z = [at(df=2 * i) for i in range(1, zn)]
    plane = [at(dy=i, dx=j) for i in range(dn) for j in range(tn) if i or j]

    barrier = pltpu.get_barrier_semaphore()
    for device in lines_x + lines_y + lines_f:
        pl.semaphore_signal(barrier, inc=1, device_id=device, device_id_type=MESH)

    first_col = (cy * y) // 128 * 128
    skip = aligned(cy * y - first_col)
    load_p = pltpu.make_async_copy(p_ref, p_v, load_sem.at[0])
    load_row = pltpu.make_async_copy(m_ref.at[pl.ds(aligned(wr * y), wr)], mrow, load_sem.at[1])
    load_col = pltpu.make_async_copy(
        m_ref.at[:, pl.ds(aligned(first_col, 128), width)], mcol, load_sem.at[2]
    )
    load_row.start()
    load_p.start()
    load_col.start()
    load_row.wait()
    load_p.wait()

    terms = jnp.zeros((3 * wr, RANK), F32)
    step = 512 if mc % 512 == 0 else 128
    for i in range(0, mc, step):
        terms = terms + dot(
            jnp.concatenate(split(mrow[:, i : i + step]), axis=0), p_v[i : i + step, :], 1, 0
        )
    wpart[...] = terms[:wr] + (terms[wr : 2 * wr] + terms[2 * wr :])

    pl.semaphore_wait(barrier, len(lines_x) + len(lines_y) + len(lines_f))

    for i, device in enumerate(lines_x):
        to = lax.rem(x + 1 + i, tn)
        send(wpart.at[pl.ds(aligned(to * br), br)], rsw.at[x], 0, device)
    rsw[x] = wpart[pl.ds(aligned(x * br), br), :]
    wait(rsw.at[pl.ds(0, tn - 1)], recv_sem.at[0])
    mine = aligned((y * tn + x) * br)
    total = rsw[0]
    for i in range(1, tn):
        total = total + rsw[i]
    wfull[pl.ds(mine, br), :] = total

    for device in plane:
        send(wfull.at[pl.ds(mine, br)], wfull.at[pl.ds(mine, br)], 1, device)
    load_col.wait()
    wait(wfull.at[pl.ds(0, mr - br)], recv_sem.at[1])

    w = wfull[...]
    gpart[...] = dot(w, w, 0, 0, HIGHEST)
    for i, device in enumerate(lines_f):
        to = lax.rem(f + 1 + i, fn)
        send(gpart.at[pl.ds(aligned(to * gr), gr)], rsg.at[f], 2, device)
    rsg[f] = gpart[pl.ds(aligned(f * gr), gr), :]

    w1, w2, w3 = split(w)
    m1, m2, m3 = split(mcol[...])
    t1 = dot(m1, jnp.concatenate([w1, w2, w3, jnp.zeros_like(w1)], axis=1), 0, 0)
    t2 = dot(m2, jnp.concatenate([w1, w2], axis=1), 0, 0)
    t3 = t1[:, 2 * RANK : 3 * RANK] + t2[:, RANK:] + dot(m3, w1, 0, 0)
    zpart[...] = t1[:, :RANK] + (t1[:, RANK : 2 * RANK] + t2[:, :RANK] + t3)
    for piece in range(2):
        for i in range(zn):
            to_z = lax.rem(z + i, zn)
            for core in range(2):
                start, length = cores[core][piece]

                def send_part(start=start, length=length, core=core, to_z=to_z, piece=piece):
                    send(
                        zpart.at[pl.ds(aligned(skip + to_z * cz + start), length)],
                        rsz.at[piece, f, pl.ds(0, length)], 3 + piece, (y, 2 * to_z + core, x),
                    )

                if i:
                    send_part()
                else:
                    pl.when(c != core)(send_part)

    wait(rsg.at[pl.ds(0, fn - 1)], recv_sem.at[2])
    total = rsg[0]
    for i in range(1, fn):
        total = total + rsg[i]
    gmine = aligned(f * gr)
    gfull[pl.ds(gmine, gr), :] = total
    for device in lines_f:
        send(gfull.at[pl.ds(gmine, gr)], gfull.at[pl.ds(gmine, gr)], 5, device)

    block = y * zn + z

    def share(core, piece):
        start, length = cores[core][piece]
        rsz[piece, f, pl.ds(0, length)] = zpart[pl.ds(aligned(skip + z * cz + start), length), :]
        wait(rsz.at[piece, pl.ds(0, fn - 1), pl.ds(0, length)], recv_sem.at[3 + piece])
        total = rsz[piece, 0, pl.ds(0, length)]
        for i in range(1, fn):
            total = total + rsz[piece, i, pl.ds(0, length)]
        zfull[block, pl.ds(start, length)] = total
        own = zfull.at[block, pl.ds(start, length)]
        for device in lines_y + lines_z:
            send(own, own, 6 + piece, device)

    even = lax.rem(y + z, 2)

    def arrived(core, piece):
        start, length = cores[core][piece]
        wait(zfull.at[pl.ds(0, dn + zn - 2), pl.ds(0, length)], recv_sem.at[6 + piece])

    def forward(core, piece):
        start, length = cores[core][piece]
        for o in range(1, dn):

            def along_z(o=o):
                ref = zfull.at[lax.rem(y + o, dn) * zn + z, pl.ds(start, length)]
                for device in lines_z:
                    send(ref, ref, 8 + piece, device)

            pl.when(even == o % 2)(along_z)
        for o in range(1, zn):

            def along_y(o=o):
                ref = zfull.at[y * zn + lax.rem(z + o, zn), pl.ds(start, length)]
                for device in lines_y:
                    send(ref, ref, 8 + piece, device)

            pl.when(even != o % 2)(along_y)

    by_core(share, 0)
    by_core(share, 1)
    wait(gfull.at[pl.ds(0, RANK - gr)], recv_sem.at[5])
    work[...] = gfull[...]
    blocks = RANK // STEP
    invert_cholesky(work, linv, 0, blocks // 2)
    by_core(arrived, 0)
    by_core(forward, 0)
    invert_cholesky(work, linv, blocks // 2, blocks)
    by_core(arrived, 1)

    def squares(core):
        (start, first), (_, second) = cores[core]
        length = first + second
        rows = [zfull[i * zn + z, pl.ds(start, length)] for i in range(dn)]
        fb = dot(jnp.concatenate(rows, axis=0), linv[...], 1, 1, HIGHEST)
        nsend[...] = jnp.sum((fb * fb).reshape(dn * length // 8, 8, RANK), axis=0)

    by_core(squares)
    for device in lines_f:
        send(nsend, nrecv.at[f], 10, device)
    nrecv[f] = nsend[...]
    by_core(forward, 1)

    left_ref[...] = dot(wfull[...], linv[...] * math.sqrt(nr), 1, 1, HIGHEST)
    l1, l2, l3 = split(jnp.transpose(linv[...]))
    factor = jnp.concatenate([l1, l2, l3, l1, l2, l1], axis=0)

    wait(nrecv.at[pl.ds(0, fn - 1)], recv_sem.at[10])
    total = nrecv[0]
    for i in range(1, fn):
        total = total + nrecv[i]
    ntotal[...] = total
    for device in lines_x:
        send(ntotal, nline.at[x], 11, device)
    nline[x] = ntotal[...]

    other = (y, f + 1 - 2 * c, x)

    def feedback(start, length):
        rows = zfull[:, pl.ds(start, length)].reshape(dn * zn * length, RANK)
        a1, a2, a3 = split(rows)
        fb = dot(jnp.concatenate([a1, a1, a1, a2, a2, a3], axis=1), factor, 1, 0)
        fb_ref[:, pl.ds(start, length)] = fb.reshape(dn * zn, length, RANK)

    def here(core, piece):
        start, length = cores[core][piece]
        wait(zfull.at[pl.ds(0, (dn - 1) * (zn - 1)), pl.ds(0, length)], recv_sem.at[8 + piece])
        part = zfull.at[:, pl.ds(start, length)]
        send(part, part, 12 + piece, other)
        feedback(start, length)

    def there(core, piece):
        start, length = cores[1 - core][piece]
        wait(zfull.at[:, pl.ds(0, length)], recv_sem.at[12 + piece])
        feedback(start, length)

    by_core(here, 0)
    by_core(there, 0)
    by_core(here, 1)

    wait(nline.at[pl.ds(0, tn - 1)], recv_sem.at[11])
    total = nline[0]
    for i in range(1, tn):
        total = total + nline[i]
    column = jnp.sqrt(jnp.sum(total, axis=0, keepdims=True) + 1e-06)
    column_ref[...] = column / math.sqrt(nc)
    scale_ref[...] = math.sqrt(nc) / column

    by_core(there, 1)

    wait(rsw.at[pl.ds(0, tn - 1)], send_sem.at[0])
    wait(wfull.at[pl.ds(0, mr - br)], send_sem.at[1])
    wait(rsg.at[pl.ds(0, fn - 1)], send_sem.at[2])
    wait(gfull.at[pl.ds(0, RANK - gr)], send_sem.at[5])
    wait(nrecv.at[pl.ds(0, fn - 1)], send_sem.at[10])
    wait(nline.at[pl.ds(0, tn - 1)], send_sem.at[11])

    def drain(core, piece):
        _, length = cores[core][piece]
        whole = zn * (cores[0][piece][1] + cores[1][piece][1])
        wait(zpart.at[pl.ds(0, whole - length)], send_sem.at[3 + piece])
        wait(zfull.at[pl.ds(0, dn + zn - 2), pl.ds(0, length)], send_sem.at[6 + piece])
        wait(zfull.at[pl.ds(0, (dn - 1) * (zn - 1)), pl.ds(0, length)], send_sem.at[8 + piece])
        wait(zfull.at[:, pl.ds(0, length)], send_sem.at[12 + piece])

    for piece in range(2):
        by_core(drain, piece)


def pieces_of(rows):
    first = (rows // 16 + 1) * 8
    out = []
    for start, length in ((0, first), (first, rows - first)):
        half = (length // 2 + 7) // 8 * 8
        out.append(((start, half), (start + half, length - half)))
    return out


def write_out(fb_ref, left_in, column_in, scale_ref, left_ref, right_ref, column_ref, rounded, sem):
    parts = rounded.shape[0]
    copies = [
        pltpu.make_async_copy(left_in, left_ref, sem.at[parts]),
        pltpu.make_async_copy(column_in, column_ref, sem.at[parts + 1]),
    ]
    for copy in copies:
        copy.start()
    n, cz, _ = fb_ref.shape
    rows = n * cz // parts
    for i in range(parts):
        part = fb_ref[pl.ds(i * n // parts, n // parts)].reshape(rows, RANK)
        rounded[i] = (part * scale_ref[...]).astype(jnp.bfloat16)
        copies.append(
            pltpu.make_async_copy(rounded.at[i], right_ref.at[pl.ds(i * rows, rows)], sem.at[i])
        )
        copies[-1].start()
    for copy in copies:
        copy.wait()


def shards(sizes, momentum, previous):
    dn, fn, tn, nr, nc = sizes
    mr, mc = momentum.shape
    wr = mr // dn
    br = wr // tn
    cy = mc // dn
    zn = fn // 2
    cz = cy // zn
    most = pieces_of(cz)[0][0][1]
    width = -(-cy // 128) * 128
    vmem = pltpu.VMEM
    whole = pl.BlockSpec(memory_space=vmem)
    hbm = pl.BlockSpec(memory_space=pl.ANY)
    left, fb, column, scale = pl.pallas_call(
        functools.partial(body, sizes),
        out_shape=(
            jax.ShapeDtypeStruct((mr, RANK), F32),
            jax.ShapeDtypeStruct((dn * zn, cz, RANK), F32),
            jax.ShapeDtypeStruct((1, RANK), F32),
            jax.ShapeDtypeStruct((1, RANK), F32),
        ),
        in_specs=[hbm] * 2,
        out_specs=(whole,) * 4,
        scratch_shapes=[
            vmem((mc, RANK), jnp.bfloat16),
            vmem((wr, mc), F32),
            vmem((mr, width), F32),
            vmem((wr, RANK), F32),
            vmem((tn, br, RANK), F32),
            vmem((mr, RANK), F32),
            vmem((RANK, RANK), F32),
            vmem((fn, RANK // fn, RANK), F32),
            vmem((RANK, RANK), F32),
            vmem((RANK, RANK), F32),
            vmem((RANK, RANK), F32),
            vmem((width, RANK), F32),
            vmem((2, fn, most, RANK), F32),
            vmem((dn * zn, cz, RANK), F32),
            vmem((8, RANK), F32),
            vmem((fn, 8, RANK), F32),
            vmem((8, RANK), F32),
            vmem((tn, 8, RANK), F32),
            pltpu.SemaphoreType.DMA((3,)),
            pltpu.SemaphoreType.DMA((14,)),
            pltpu.SemaphoreType.DMA((14,)),
        ],
        compiler_params=pltpu.CompilerParams(
            collective_id=0, has_side_effects=True, vmem_limit_bytes=LIMIT
        ),
    )(momentum, previous)
    parts = 4 if dn * zn % 4 == 0 and dn * zn * cz // 4 % 16 == 0 else 1
    left, right, column = pl.pallas_call(
        write_out,
        out_shape=(
            jax.ShapeDtypeStruct((mr, RANK), F32),
            jax.ShapeDtypeStruct((mc, RANK), jnp.bfloat16),
            jax.ShapeDtypeStruct((1, RANK), F32),
        ),
        in_specs=[whole] * 4,
        out_specs=(hbm,) * 3,
        scratch_shapes=[
            vmem((parts, mc // parts, RANK), jnp.bfloat16),
            pltpu.SemaphoreType.DMA((parts + 2,)),
        ],
        compiler_params=pltpu.CompilerParams(vmem_limit_bytes=16 * 2**20),
    )(fb, left, column, scale)
    return left, right, column.reshape(RANK)


def solution(mesh):
    dn, fn, tn = (mesh.shape[name] for name in ("dp", "fsdp", "tensor"))

    def run(momentum, previous):
        sizes = (dn, fn, tn, momentum.shape[0], momentum.shape[1])
        return jax.shard_map(
            functools.partial(shards, sizes),
            mesh=mesh,
            in_specs=(P("fsdp", "tensor"), P("tensor", None)),
            out_specs=(P("fsdp", None), P("tensor", None), P()),
            check_vma=False,
        )(momentum, previous)

    return run
```

```python
import functools
import math

import jax
import jax.numpy as jnp
from jax import lax
from jax.experimental import pallas as pl
from jax.experimental.pallas import tpu as pltpu
from jax.sharding import PartitionSpec as P

HIGHEST = lax.Precision.HIGHEST
MESH = pl.DeviceIdType.MESH
LIMIT = 51 * 2**20
RANK = 128
F32 = jnp.float32


def aligned(value, multiple=8):
    return pl.multiple_of(value, multiple)


STEP = 16


def split(v):
    first = v.astype(jnp.bfloat16)
    rest = v - first.astype(F32)
    second = rest.astype(jnp.bfloat16)
    return first, second, (rest - second.astype(F32)).astype(jnp.bfloat16)


def dot(a, b, ca, cb, precision=None):
    return lax.dot_general(
        a, b, (((ca,), (cb,)), ((), ())), precision=precision, preferred_element_type=F32
    )


def invert_cholesky(a_ref, linv_ref, first, last):
    shape = (STEP, RANK)
    sub = lax.broadcasted_iota(jnp.int32, shape, 0)
    lane = lax.broadcasted_iota(jnp.int32, shape, 1)
    row = lax.broadcasted_iota(jnp.int32, (RANK, RANK), 0)
    col = lax.broadcasted_iota(jnp.int32, (RANK, RANK), 1)

    def row_of(v, p):
        return jnp.broadcast_to(v[p : p + 1, :], shape)

    def block(k, carry):
        off = aligned(k * STEP, STEP)
        rows = a_ref[pl.ds(off, STEP), :]
        turned = pltpu.roll(rows, lax.rem(RANK - off, RANK), 1)
        cols = [jnp.broadcast_to(turned[:, q : q + 1], shape) for q in range(STEP)]
        rel = lane - off
        scale = jnp.zeros(shape, F32)
        for p in range(STEP):
            pivot = row_of(cols[p], p)
            factor = jnp.where(sub > p, cols[p] * (1.0 / pivot), 0.0)
            pivot_row = row_of(rows, p)
            for q in range(p + 1, STEP):
                cols[q] = cols[q] - factor * row_of(cols[q], p)
            rows = jnp.where((rel == p) & (sub > p), 0.0, rows) - factor * jnp.where(rel == p, 1.0, pivot_row)
            scale = jnp.where(sub == p, lax.rsqrt(pivot), scale)
        panel = jnp.where(rel == sub, 1.0, rows) * scale
        panel = jnp.where((rel > sub) & (rel < STEP), 0.0, panel)
        linv_ref[pl.ds(off, STEP), :] = jnp.where(rel <= sub, panel, 0.0)
        upper = jnp.where(rel >= STEP, panel, 0.0)
        u1, u2, u3 = split(upper)
        p1, p2, p3 = split(panel)
        update = dot(
            jnp.concatenate([u1, u1, u1, u2, u2, u3], axis=0),
            jnp.concatenate([p1, p2, p3, p1, p2, p1], axis=0), 0, 0,
        )
        a = a_ref[...]
        inside = (col >= off) & (col < off + STEP)
        a_ref[...] = jnp.where(row >= off + STEP, jnp.where(inside, 0.0, a) - update, a)
        return carry

    lax.fori_loop(first, last, block, 0)


def body(
    sizes, m_ref, p_ref, left_ref, fb_ref, column_ref, scale_ref,
    p_v, mrow, mcol, turned, wpart, rsw, wfull, gpart, rsg, gfull, work, linv, zpart, rsz, zfull, nsend, nrecv, ntotal, nline,
    load_sem, send_sem, recv_sem,
):
    dn, fn, tn, nr, nc = sizes
    zn = fn // 2
    mr, mc = m_ref.shape
    wr = mr // dn
    br = wr // tn
    cy = mc // dn
    cz = cy // zn
    cores = pieces_of(cz)
    gr = RANK // fn
    width = mcol.shape[1]
    y, f, x = lax.axis_index("dp"), lax.axis_index("fsdp"), lax.axis_index("tensor")
    z, c = f // 2, lax.rem(f, 2)

    def at(dy=0, df=0, dx=0):
        return (lax.rem(y + dy, dn), lax.rem(f + df, fn), lax.rem(x + dx, tn))

    def send(src, dst, phase, device):
        pltpu.make_async_remote_copy(
            src_ref=src, dst_ref=dst, send_sem=send_sem.at[phase], recv_sem=recv_sem.at[phase],
            device_id=device, device_id_type=MESH,
        ).start()

    def wait(ref, sem):
        pltpu.make_async_copy(ref, ref, sem).wait()

    def by_core(fun, *args):
        for core in range(2):
            pl.when(c == core)(functools.partial(fun, core, *args))

    def far_first(n):
        return sorted(range(1, n), key=lambda i: -min(i, n - i))

    lines_x = [at(dx=i) for i in far_first(tn)]
    lines_y = [at(dy=i) for i in far_first(dn)]
    lines_f = [at(df=i) for i in far_first(fn)]
    lines_z = [at(df=2 * i) for i in far_first(zn)]
    plane = [(i, j) for i in range(dn) for j in range(tn) if i or j]
    plane.sort(key=lambda ij: -(min(ij[0], dn - ij[0]) + min(ij[1], tn - ij[1])))
    plane = [at(dy=i, dx=j) for i, j in plane]

    barrier = pltpu.get_barrier_semaphore()
    for device in lines_x + lines_y + lines_f:
        pl.semaphore_signal(barrier, inc=1, device_id=device, device_id_type=MESH)

    first_col = (cy * y) // 128 * 128
    skip = aligned(cy * y - first_col)
    step = mc // 7
    loads = []
    for i in range(7):
        part = pl.ds(i * step, step)
        row = m_ref.at[pl.ds(aligned(wr * y), wr), part]
        loads.append(
            (
                pltpu.make_async_copy(row, mrow.at[:, part], load_sem.at[2 * i]),
                pltpu.make_async_copy(p_ref.at[part], p_v.at[part], load_sem.at[2 * i + 1]),
            )
        )
        for load in loads[i]:
            load.start()
    load_col = pltpu.make_async_copy(
        m_ref.at[:, pl.ds(aligned(first_col, 128), width)], mcol, load_sem.at[14]
    )
    load_col.start()

    terms = jnp.zeros((3 * wr, RANK), F32)
    for i in range(7):
        for load in loads[i]:
            load.wait()
        part = slice(i * step, (i + 1) * step)
        terms = terms + dot(jnp.concatenate(split(mrow[:, part]), axis=0), p_v[part, :], 1, 0)
    wpart[...] = terms[:wr] + (terms[wr : 2 * wr] + terms[2 * wr :])

    pl.semaphore_wait(barrier, len(lines_x) + len(lines_y) + len(lines_f))

    for device in lines_x:
        to = device[2]
        send(wpart.at[pl.ds(aligned(to * br), br)], rsw.at[x], 0, device)
    rsw[x] = wpart[pl.ds(aligned(x * br), br), :]
    wait(rsw.at[pl.ds(0, tn - 1)], recv_sem.at[0])
    mine = aligned((y * tn + x) * br)
    total = rsw[0]
    for i in range(1, tn):
        total = total + rsw[i]
    wfull[pl.ds(mine, br), :] = total

    for device in plane:
        send(wfull.at[pl.ds(mine, br)], wfull.at[pl.ds(mine, br)], 1, device)
    load_col.wait()
    for i, term in enumerate(split(jnp.transpose(mcol[...]))):
        turned[i] = term
    wait(wfull.at[pl.ds(0, mr - br)], recv_sem.at[1])

    w = wfull[...]
    w1, w2, w3 = split(w)
    t1 = dot(w1, jnp.concatenate([w1, w2, w3, w2], axis=1), 0, 0)
    t2 = t1[:, RANK : 2 * RANK] + t1[:, 2 * RANK : 3 * RANK]
    gpart[...] = t1[:, :RANK] + (t2 + jnp.transpose(t2) + dot(w2, w2, 0, 0))
    for device in lines_f:
        to = device[1]
        send(gpart.at[pl.ds(aligned(to * gr), gr)], rsg.at[f], 2, device)
    rsg[f] = gpart[pl.ds(aligned(f * gr), gr), :]

    t1 = dot(turned[0], jnp.concatenate([w1, w2, w3, jnp.zeros_like(w1)], axis=1), 1, 0)
    t2 = dot(turned[1], jnp.concatenate([w1, w2], axis=1), 1, 0)
    t3 = t1[:, 2 * RANK : 3 * RANK] + t2[:, RANK:] + dot(turned[2], w1, 1, 0)
    zpart[...] = t1[:, :RANK] + (t1[:, RANK : 2 * RANK] + t2[:, :RANK] + t3)
    for piece in range(2):
        for i in far_first(zn) + [0]:
            to_z = lax.rem(z + i, zn)
            for core in range(2):
                start, length = cores[core][piece]

                def send_part(start=start, length=length, core=core, to_z=to_z, piece=piece):
                    send(
                        zpart.at[pl.ds(aligned(skip + to_z * cz + start), length)],
                        rsz.at[piece, f, pl.ds(0, length)], 3 + piece, (y, 2 * to_z + core, x),
                    )

                if i:
                    send_part()
                else:
                    pl.when(c != core)(send_part)

    wait(rsg.at[pl.ds(0, fn - 1)], recv_sem.at[2])
    total = rsg[0]
    for i in range(1, fn):
        total = total + rsg[i]
    gmine = aligned(f * gr)
    gfull[pl.ds(gmine, gr), :] = total
    for device in lines_f:
        send(gfull.at[pl.ds(gmine, gr)], gfull.at[pl.ds(gmine, gr)], 5, device)

    block = y * zn + z

    def share(core, piece):
        start, length = cores[core][piece]
        rsz[piece, f, pl.ds(0, length)] = zpart[pl.ds(aligned(skip + z * cz + start), length), :]
        wait(rsz.at[piece, pl.ds(0, fn - 1), pl.ds(0, length)], recv_sem.at[3 + piece])
        total = rsz[piece, 0, pl.ds(0, length)]
        for i in range(1, fn):
            total = total + rsz[piece, i, pl.ds(0, length)]
        zfull[block, pl.ds(start, length)] = total
        own = zfull.at[block, pl.ds(start, length)]
        for device in lines_y + lines_z:
            send(own, own, 6 + piece, device)

    even = lax.rem(y + z, 2)

    def arrived(core, piece):
        start, length = cores[core][piece]
        wait(zfull.at[pl.ds(0, dn + zn - 2), pl.ds(0, length)], recv_sem.at[6 + piece])

    def forward(core, piece):
        start, length = cores[core][piece]
        for o in range(1, dn):

            def along_z(o=o):
                ref = zfull.at[lax.rem(y + o, dn) * zn + z, pl.ds(start, length)]
                for device in lines_z:
                    send(ref, ref, 8 + piece, device)

            pl.when(even == o % 2)(along_z)
        for o in range(1, zn):

            def along_y(o=o):
                ref = zfull.at[y * zn + lax.rem(z + o, zn), pl.ds(start, length)]
                for device in lines_y:
                    send(ref, ref, 8 + piece, device)

            pl.when(even != o % 2)(along_y)

    by_core(share, 0)
    by_core(share, 1)
    wait(gfull.at[pl.ds(0, RANK - gr)], recv_sem.at[5])
    work[...] = gfull[...]
    blocks = RANK // STEP
    invert_cholesky(work, linv, 0, blocks // 2)
    by_core(arrived, 0)
    by_core(forward, 0)
    invert_cholesky(work, linv, blocks // 2, blocks)
    by_core(arrived, 1)

    def squares(core):
        (start, first), (_, second) = cores[core]
        length = first + second
        rows = [zfull[i * zn + z, pl.ds(start, length)] for i in range(dn)]
        fb = dot(jnp.concatenate(rows, axis=0), linv[...], 1, 1, HIGHEST)
        nsend[...] = jnp.sum((fb * fb).reshape(dn * length // 8, 8, RANK), axis=0)

    by_core(squares)
    for device in lines_f:
        send(nsend, nrecv.at[f], 10, device)
    nrecv[f] = nsend[...]
    by_core(forward, 1)

    left_ref[...] = dot(wfull[...], linv[...] * math.sqrt(nr), 1, 1, HIGHEST)
    l1, l2, l3 = split(jnp.transpose(linv[...]))
    factor = jnp.concatenate([l1, l2, l3, l1, l2, l1], axis=0)

    wait(nrecv.at[pl.ds(0, fn - 1)], recv_sem.at[10])
    total = nrecv[0]
    for i in range(1, fn):
        total = total + nrecv[i]
    ntotal[...] = total
    for device in lines_x:
        send(ntotal, nline.at[x], 11, device)
    nline[x] = ntotal[...]

    other = (y, f + 1 - 2 * c, x)

    def feedback(start, length):
        rows = zfull[:, pl.ds(start, length)].reshape(dn * zn * length, RANK)
        a1, a2, a3 = split(rows)
        fb = dot(jnp.concatenate([a1, a1, a1, a2, a2, a3], axis=1), factor, 1, 0)
        fb_ref[:, pl.ds(start, length)] = fb.reshape(dn * zn, length, RANK)

    def here(core, piece):
        start, length = cores[core][piece]
        wait(zfull.at[pl.ds(0, (dn - 1) * (zn - 1)), pl.ds(0, length)], recv_sem.at[8 + piece])
        part = zfull.at[:, pl.ds(start, length)]
        send(part, part, 12 + piece, other)
        feedback(start, length)

    def there(core, piece):
        start, length = cores[1 - core][piece]
        wait(zfull.at[:, pl.ds(0, length)], recv_sem.at[12 + piece])
        feedback(start, length)

    by_core(here, 0)
    by_core(there, 0)
    by_core(here, 1)

    wait(nline.at[pl.ds(0, tn - 1)], recv_sem.at[11])
    total = nline[0]
    for i in range(1, tn):
        total = total + nline[i]
    column = jnp.sqrt(jnp.sum(total, axis=0, keepdims=True) + 1e-06)
    column_ref[...] = column / math.sqrt(nc)
    scale_ref[...] = math.sqrt(nc) / column

    by_core(there, 1)

    wait(rsw.at[pl.ds(0, tn - 1)], send_sem.at[0])
    wait(wfull.at[pl.ds(0, mr - br)], send_sem.at[1])
    wait(rsg.at[pl.ds(0, fn - 1)], send_sem.at[2])
    wait(gfull.at[pl.ds(0, RANK - gr)], send_sem.at[5])
    wait(nrecv.at[pl.ds(0, fn - 1)], send_sem.at[10])
    wait(nline.at[pl.ds(0, tn - 1)], send_sem.at[11])

    def drain(core, piece):
        _, length = cores[core][piece]
        whole = zn * (cores[0][piece][1] + cores[1][piece][1])
        wait(zpart.at[pl.ds(0, whole - length)], send_sem.at[3 + piece])
        wait(zfull.at[pl.ds(0, dn + zn - 2), pl.ds(0, length)], send_sem.at[6 + piece])
        wait(zfull.at[pl.ds(0, (dn - 1) * (zn - 1)), pl.ds(0, length)], send_sem.at[8 + piece])
        wait(zfull.at[:, pl.ds(0, length)], send_sem.at[12 + piece])

    for piece in range(2):
        by_core(drain, piece)


def pieces_of(rows):
    first = (rows // 16 + 1) * 8
    out = []
    for start, length in ((0, first), (first, rows - first)):
        half = (length // 2 + 7) // 8 * 8
        out.append(((start, half), (start + half, length - half)))
    return out


def write_out(fb_ref, left_in, column_in, scale_ref, left_ref, right_ref, column_ref, rounded, sem):
    parts = rounded.shape[0]
    copies = [
        pltpu.make_async_copy(left_in, left_ref, sem.at[parts]),
        pltpu.make_async_copy(column_in, column_ref, sem.at[parts + 1]),
    ]
    for copy in copies:
        copy.start()
    n, cz, _ = fb_ref.shape
    rows = n * cz // parts
    for i in range(parts):
        part = fb_ref[pl.ds(i * n // parts, n // parts)].reshape(rows, RANK)
        rounded[i] = (part * scale_ref[...]).astype(jnp.bfloat16)
        copies.append(
            pltpu.make_async_copy(rounded.at[i], right_ref.at[pl.ds(i * rows, rows)], sem.at[i])
        )
        copies[-1].start()
    for copy in copies:
        copy.wait()


def shards(sizes, momentum, previous):
    dn, fn, tn, nr, nc = sizes
    mr, mc = momentum.shape
    wr = mr // dn
    br = wr // tn
    cy = mc // dn
    zn = fn // 2
    cz = cy // zn
    most = pieces_of(cz)[0][0][1]
    width = -(-cy // 128) * 128
    vmem = pltpu.VMEM
    whole = pl.BlockSpec(memory_space=vmem)
    hbm = pl.BlockSpec(memory_space=pl.ANY)
    left, fb, column, scale = pl.pallas_call(
        functools.partial(body, sizes),
        out_shape=(
            jax.ShapeDtypeStruct((mr, RANK), F32),
            jax.ShapeDtypeStruct((dn * zn, cz, RANK), F32),
            jax.ShapeDtypeStruct((1, RANK), F32),
            jax.ShapeDtypeStruct((1, RANK), F32),
        ),
        in_specs=[pl.BlockSpec(memory_space=pltpu.HBM)] * 2,
        out_specs=(whole,) * 4,
        scratch_shapes=[
            vmem((mc, RANK), jnp.bfloat16),
            vmem((wr, mc), F32),
            vmem((mr, width), F32),
            vmem((3, width, mr), jnp.bfloat16),
            vmem((wr, RANK), F32),
            vmem((tn, br, RANK), F32),
            vmem((mr, RANK), F32),
            vmem((RANK, RANK), F32),
            vmem((fn, RANK // fn, RANK), F32),
            vmem((RANK, RANK), F32),
            vmem((RANK, RANK), F32),
            vmem((RANK, RANK), F32),
            vmem((width, RANK), F32),
            vmem((2, fn, most, RANK), F32),
            vmem((dn * zn, cz, RANK), F32),
            vmem((8, RANK), F32),
            vmem((fn, 8, RANK), F32),
            vmem((8, RANK), F32),
            vmem((tn, 8, RANK), F32),
            pltpu.SemaphoreType.DMA((15,)),
            pltpu.SemaphoreType.DMA((14,)),
            pltpu.SemaphoreType.DMA((14,)),
        ],
        compiler_params=pltpu.CompilerParams(
            collective_id=0, has_side_effects=True, vmem_limit_bytes=LIMIT
        ),
    )(pltpu.with_memory_space_constraint(momentum, pltpu.HBM), pltpu.with_memory_space_constraint(previous, pltpu.HBM))
    parts = 4 if dn * zn % 4 == 0 and dn * zn * cz // 4 % 16 == 0 else 1
    left, right, column = pl.pallas_call(
        write_out,
        out_shape=(
            jax.ShapeDtypeStruct((mr, RANK), F32),
            jax.ShapeDtypeStruct((mc, RANK), jnp.bfloat16),
            jax.ShapeDtypeStruct((1, RANK), F32),
        ),
        in_specs=[whole] * 4,
        out_specs=(hbm,) * 3,
        scratch_shapes=[
            vmem((parts, mc // parts, RANK), jnp.bfloat16),
            pltpu.SemaphoreType.DMA((parts + 2,)),
        ],
        compiler_params=pltpu.CompilerParams(vmem_limit_bytes=16 * 2**20),
    )(fb, left, column, scale)
    return left, right, column.reshape(RANK)


def solution(mesh):
    dn, fn, tn = (mesh.shape[name] for name in ("dp", "fsdp", "tensor"))

    def run(momentum, previous):
        sizes = (dn, fn, tn, momentum.shape[0], momentum.shape[1])
        return jax.shard_map(
            functools.partial(shards, sizes),
            mesh=mesh,
            in_specs=(P("fsdp", "tensor"), P("tensor", None)),
            out_specs=(P("fsdp", None), P("tensor", None), P()),
            check_vma=False,
        )(momentum, previous)

    return run
```

```python
import functools
import math

import jax
import jax.numpy as jnp
from jax import lax
from jax.experimental import pallas as pl
from jax.experimental.pallas import tpu as pltpu
from jax.sharding import PartitionSpec as P

HIGHEST = lax.Precision.HIGHEST
MESH = pl.DeviceIdType.MESH
LIMIT = 51 * 2**20
RANK = 128
F32 = jnp.float32


def aligned(value, multiple=8):
    return pl.multiple_of(value, multiple)


STEP = 16


def split(v):
    first = v.astype(jnp.bfloat16)
    rest = v - first.astype(F32)
    second = rest.astype(jnp.bfloat16)
    return first, second, (rest - second.astype(F32)).astype(jnp.bfloat16)


def dot(a, b, ca, cb, precision=None):
    return lax.dot_general(
        a, b, (((ca,), (cb,)), ((), ())), precision=precision, preferred_element_type=F32
    )


def invert_cholesky(a_ref, linv_ref, first, last):
    shape = (STEP, RANK)
    sub = lax.broadcasted_iota(jnp.int32, shape, 0)
    lane = lax.broadcasted_iota(jnp.int32, shape, 1)
    row = lax.broadcasted_iota(jnp.int32, (RANK, RANK), 0)
    col = lax.broadcasted_iota(jnp.int32, (RANK, RANK), 1)

    def row_of(v, p):
        return jnp.broadcast_to(v[p : p + 1, :], shape)

    def block(k, carry):
        off = aligned(k * STEP, STEP)
        rows = a_ref[pl.ds(off, STEP), :]
        turned = pltpu.roll(rows, lax.rem(RANK - off, RANK), 1)
        cols = [jnp.broadcast_to(turned[:, q : q + 1], shape) for q in range(STEP)]
        rel = lane - off
        scale = jnp.zeros(shape, F32)
        for p in range(STEP):
            pivot = row_of(cols[p], p)
            factor = jnp.where(sub > p, cols[p] * (1.0 / pivot), 0.0)
            pivot_row = row_of(rows, p)
            for q in range(p + 1, STEP):
                cols[q] = cols[q] - factor * row_of(cols[q], p)
            rows = jnp.where((rel == p) & (sub > p), 0.0, rows) - factor * jnp.where(rel == p, 1.0, pivot_row)
            scale = jnp.where(sub == p, lax.rsqrt(pivot), scale)
        panel = jnp.where(rel == sub, 1.0, rows) * scale
        panel = jnp.where((rel > sub) & (rel < STEP), 0.0, panel)
        linv_ref[pl.ds(off, STEP), :] = jnp.where(rel <= sub, panel, 0.0)
        upper = jnp.where(rel >= STEP, panel, 0.0)
        u1, u2, u3 = split(upper)
        p1, p2, p3 = split(panel)
        update = dot(
            jnp.concatenate([u1, u1, u1, u2, u2, u3], axis=0),
            jnp.concatenate([p1, p2, p3, p1, p2, p1], axis=0), 0, 0,
        )
        a = a_ref[...]
        inside = (col >= off) & (col < off + STEP)
        a_ref[...] = jnp.where(row >= off + STEP, jnp.where(inside, 0.0, a) - update, a)
        return carry

    lax.fori_loop(first, last, block, 0)


def body(
    sizes, m_ref, p_ref, left_ref, fb_ref, column_ref, scale_ref,
    p_v, mrow, mcol, turned, wpart, rsw, wfull, gpart, rsg, gfull, work, linv, zpart, rsz, zfull, nsend, nrecv, ntotal, nline,
    load_sem, send_sem, recv_sem,
):
    dn, fn, tn, nr, nc = sizes
    zn = fn // 2
    mr, mc = m_ref.shape
    wr = mr // dn
    br = wr // tn
    cy = mc // dn
    cz = cy // zn
    cores = pieces_of(cz)
    gr = RANK // fn
    width = mcol.shape[1]
    y, f, x = lax.axis_index("dp"), lax.axis_index("fsdp"), lax.axis_index("tensor")
    z, c = f // 2, lax.rem(f, 2)

    def at(dy=0, df=0, dx=0):
        return (lax.rem(y + dy, dn), lax.rem(f + df, fn), lax.rem(x + dx, tn))

    def send(src, dst, phase, device):
        pltpu.make_async_remote_copy(
            src_ref=src, dst_ref=dst, send_sem=send_sem.at[phase], recv_sem=recv_sem.at[phase],
            device_id=device, device_id_type=MESH,
        ).start()

    def wait(ref, sem):
        pltpu.make_async_copy(ref, ref, sem).wait()

    def by_core(fun, *args):
        for core in range(2):
            pl.when(c == core)(functools.partial(fun, core, *args))

    def far_first(n):
        return sorted(range(1, n), key=lambda i: -min(i, n - i))

    lines_x = [at(dx=i) for i in far_first(tn)]
    lines_y = [at(dy=i) for i in far_first(dn)]
    lines_f = [at(df=i) for i in far_first(fn)]
    lines_z = [at(df=2 * i) for i in far_first(zn)]
    plane = [(i, j) for i in range(dn) for j in range(tn) if i or j]
    plane.sort(key=lambda ij: -(min(ij[0], dn - ij[0]) + min(ij[1], tn - ij[1])))
    plane = [at(dy=i, dx=j) for i, j in plane]

    barrier = pltpu.get_barrier_semaphore()
    for device in lines_x + lines_y + lines_f:
        pl.semaphore_signal(barrier, inc=1, device_id=device, device_id_type=MESH)

    first_col = (cy * y) // 128 * 128
    skip = aligned(cy * y - first_col)
    step = mc // 7
    loads = []
    for i in range(7):
        part = pl.ds(i * step, step)
        row = m_ref.at[pl.ds(aligned(wr * y), wr), part]
        loads.append(
            (
                pltpu.make_async_copy(row, mrow.at[:, part], load_sem.at[2 * i]),
                pltpu.make_async_copy(p_ref.at[part], p_v.at[part], load_sem.at[2 * i + 1]),
            )
        )
        for load in loads[i]:
            load.start()
    load_col = pltpu.make_async_copy(
        m_ref.at[:, pl.ds(aligned(first_col, 128), width)], mcol, load_sem.at[14]
    )
    load_col.start()

    terms = jnp.zeros((3 * wr, RANK), F32)
    for i in range(7):
        for load in loads[i]:
            load.wait()
        part = slice(i * step, (i + 1) * step)
        terms = terms + dot(jnp.concatenate(split(mrow[:, part]), axis=0), p_v[part, :], 1, 0)
    wpart[...] = terms[:wr] + (terms[wr : 2 * wr] + terms[2 * wr :])

    pl.semaphore_wait(barrier, len(lines_x) + len(lines_y) + len(lines_f))

    for device in lines_x:
        to = device[2]
        send(wpart.at[pl.ds(aligned(to * br), br)], rsw.at[x], 0, device)
    rsw[x] = wpart[pl.ds(aligned(x * br), br), :]
    wait(rsw.at[pl.ds(0, tn - 1)], recv_sem.at[0])
    mine = aligned((y * tn + x) * br)
    total = rsw[0]
    for i in range(1, tn):
        total = total + rsw[i]
    wfull[pl.ds(mine, br), :] = total

    for device in plane:
        send(wfull.at[pl.ds(mine, br)], wfull.at[pl.ds(mine, br)], 1, device)
    load_col.wait()
    for i, term in enumerate(split(jnp.transpose(mcol[...]))):
        turned[i] = term
    wait(wfull.at[pl.ds(0, mr - br)], recv_sem.at[1])

    w = wfull[...]
    w1, w2, w3 = split(w)
    t1 = dot(w1, jnp.concatenate([w1, w2, w3, w2], axis=1), 0, 0)
    t2 = t1[:, RANK : 2 * RANK] + t1[:, 2 * RANK : 3 * RANK]
    gpart[...] = t1[:, :RANK] + (t2 + jnp.transpose(t2) + dot(w2, w2, 0, 0))
    for device in lines_f:
        to = device[1]
        send(gpart.at[pl.ds(aligned(to * gr), gr)], rsg.at[f], 2, device)
    rsg[f] = gpart[pl.ds(aligned(f * gr), gr), :]

    t1 = dot(turned[0], jnp.concatenate([w1, w2, w3, jnp.zeros_like(w1)], axis=1), 1, 0)
    t2 = dot(turned[1], jnp.concatenate([w1, w2], axis=1), 1, 0)
    t3 = t1[:, 2 * RANK : 3 * RANK] + t2[:, RANK:] + dot(turned[2], w1, 1, 0)
    zpart[...] = t1[:, :RANK] + (t1[:, RANK : 2 * RANK] + t2[:, :RANK] + t3)
    for piece in range(2):
        for i in far_first(zn) + [0]:
            to_z = lax.rem(z + i, zn)
            for core in range(2):
                start, length = cores[core][piece]

                def send_part(start=start, length=length, core=core, to_z=to_z, piece=piece):
                    send(
                        zpart.at[pl.ds(aligned(skip + to_z * cz + start), length)],
                        rsz.at[piece, f, pl.ds(0, length)], 3 + piece, (y, 2 * to_z + core, x),
                    )

                if i:
                    send_part()
                else:
                    pl.when(c != core)(send_part)

    wait(rsg.at[pl.ds(0, fn - 1)], recv_sem.at[2])
    total = rsg[0]
    for i in range(1, fn):
        total = total + rsg[i]
    gmine = aligned(f * gr)
    gfull[pl.ds(gmine, gr), :] = total
    for device in lines_f:
        send(gfull.at[pl.ds(gmine, gr)], gfull.at[pl.ds(gmine, gr)], 5, device)

    block = y * zn + z

    def share(core, piece):
        start, length = cores[core][piece]
        rsz[piece, f, pl.ds(0, length)] = zpart[pl.ds(aligned(skip + z * cz + start), length), :]
        wait(rsz.at[piece, pl.ds(0, fn - 1), pl.ds(0, length)], recv_sem.at[3 + piece])
        total = rsz[piece, 0, pl.ds(0, length)]
        for i in range(1, fn):
            total = total + rsz[piece, i, pl.ds(0, length)]
        zfull[block, pl.ds(start, length)] = total
        own = zfull.at[block, pl.ds(start, length)]
        for device in lines_y + lines_z:
            send(own, own, 6 + piece, device)

    even = lax.rem(y + z, 2)

    def arrived(core, piece):
        start, length = cores[core][piece]
        wait(zfull.at[pl.ds(0, dn + zn - 2), pl.ds(0, length)], recv_sem.at[6 + piece])

    def forward(core, piece):
        start, length = cores[core][piece]
        for o in range(1, dn):

            def along_z(o=o):
                ref = zfull.at[lax.rem(y + o, dn) * zn + z, pl.ds(start, length)]
                for device in lines_z:
                    send(ref, ref, 8 + piece, device)

            pl.when(even == o % 2)(along_z)
        for o in range(1, zn):

            def along_y(o=o):
                ref = zfull.at[y * zn + lax.rem(z + o, zn), pl.ds(start, length)]
                for device in lines_y:
                    send(ref, ref, 8 + piece, device)

            pl.when(even != o % 2)(along_y)

    by_core(share, 0)
    by_core(share, 1)
    wait(gfull.at[pl.ds(0, RANK - gr)], recv_sem.at[5])
    work[...] = gfull[...]
    blocks = RANK // STEP
    invert_cholesky(work, linv, 0, blocks // 2)
    by_core(arrived, 0)
    by_core(forward, 0)
    invert_cholesky(work, linv, blocks // 2, blocks)
    by_core(arrived, 1)

    def squares(core):
        (start, first), (_, second) = cores[core]
        length = first + second
        rows = [zfull[i * zn + z, pl.ds(start, length)] for i in range(dn)]
        fb = dot(jnp.concatenate(rows, axis=0), linv[...], 1, 1, HIGHEST)
        nsend[...] = jnp.sum((fb * fb).reshape(dn * length // 8, 8, RANK), axis=0)

    by_core(squares)
    for device in lines_x:
        send(nsend, nline.at[x], 11, device)
    nline[x] = nsend[...]
    by_core(forward, 1)

    left_ref[...] = dot(wfull[...], linv[...] * math.sqrt(nr), 1, 1, HIGHEST)
    l1, l2, l3 = split(jnp.transpose(linv[...]))
    factor = jnp.concatenate([l1, l2, l3, l1, l2, l1], axis=0)

    wait(nline.at[pl.ds(0, tn - 1)], recv_sem.at[11])
    total = nline[0]
    for i in range(1, tn):
        total = total + nline[i]
    ntotal[...] = total
    for device in lines_f:
        send(ntotal, nrecv.at[f], 10, device)
    nrecv[f] = ntotal[...]

    other = (y, f + 1 - 2 * c, x)

    def feedback(start, length):
        rows = zfull[:, pl.ds(start, length)].reshape(dn * zn * length, RANK)
        a1, a2, a3 = split(rows)
        fb = dot(jnp.concatenate([a1, a1, a1, a2, a2, a3], axis=1), factor, 1, 0)
        fb_ref[:, pl.ds(start, length)] = fb.reshape(dn * zn, length, RANK)

    def here(core, piece):
        start, length = cores[core][piece]
        wait(zfull.at[pl.ds(0, (dn - 1) * (zn - 1)), pl.ds(0, length)], recv_sem.at[8 + piece])
        part = zfull.at[:, pl.ds(start, length)]
        send(part, part, 12 + piece, other)
        feedback(start, length)

    def there(core, piece):
        start, length = cores[1 - core][piece]
        wait(zfull.at[:, pl.ds(0, length)], recv_sem.at[12 + piece])
        feedback(start, length)

    by_core(here, 0)
    by_core(there, 0)
    by_core(here, 1)

    wait(nrecv.at[pl.ds(0, fn - 1)], recv_sem.at[10])
    total = nrecv[0]
    for i in range(1, fn):
        total = total + nrecv[i]
    column = jnp.sqrt(jnp.sum(total, axis=0, keepdims=True) + 1e-06)
    column_ref[...] = column / math.sqrt(nc)
    scale_ref[...] = math.sqrt(nc) / column

    by_core(there, 1)

    wait(rsw.at[pl.ds(0, tn - 1)], send_sem.at[0])
    wait(wfull.at[pl.ds(0, mr - br)], send_sem.at[1])
    wait(rsg.at[pl.ds(0, fn - 1)], send_sem.at[2])
    wait(gfull.at[pl.ds(0, RANK - gr)], send_sem.at[5])
    wait(nrecv.at[pl.ds(0, fn - 1)], send_sem.at[10])
    wait(nline.at[pl.ds(0, tn - 1)], send_sem.at[11])

    def drain(core, piece):
        _, length = cores[core][piece]
        whole = zn * (cores[0][piece][1] + cores[1][piece][1])
        wait(zpart.at[pl.ds(0, whole - length)], send_sem.at[3 + piece])
        wait(zfull.at[pl.ds(0, dn + zn - 2), pl.ds(0, length)], send_sem.at[6 + piece])
        wait(zfull.at[pl.ds(0, (dn - 1) * (zn - 1)), pl.ds(0, length)], send_sem.at[8 + piece])
        wait(zfull.at[:, pl.ds(0, length)], send_sem.at[12 + piece])

    for piece in range(2):
        by_core(drain, piece)


def pieces_of(rows):
    first = (rows // 16 + 1) * 8
    out = []
    for start, length in ((0, first), (first, rows - first)):
        half = (length // 2 + 7) // 8 * 8
        out.append(((start, half), (start + half, length - half)))
    return out


def write_out(fb_ref, left_in, column_in, scale_ref, left_ref, right_ref, column_ref, rounded, sem):
    parts = rounded.shape[0]
    copies = [
        pltpu.make_async_copy(left_in, left_ref, sem.at[parts]),
        pltpu.make_async_copy(column_in, column_ref, sem.at[parts + 1]),
    ]
    for copy in copies:
        copy.start()
    n, cz, _ = fb_ref.shape
    rows = n * cz // parts
    for i in range(parts):
        part = fb_ref[pl.ds(i * n // parts, n // parts)].reshape(rows, RANK)
        rounded[i] = (part * scale_ref[...]).astype(jnp.bfloat16)
        copies.append(
            pltpu.make_async_copy(rounded.at[i], right_ref.at[pl.ds(i * rows, rows)], sem.at[i])
        )
        copies[-1].start()
    for copy in copies:
        copy.wait()


def shards(sizes, momentum, previous):
    dn, fn, tn, nr, nc = sizes
    mr, mc = momentum.shape
    wr = mr // dn
    br = wr // tn
    cy = mc // dn
    zn = fn // 2
    cz = cy // zn
    most = pieces_of(cz)[0][0][1]
    width = -(-cy // 128) * 128
    vmem = pltpu.VMEM
    whole = pl.BlockSpec(memory_space=vmem)
    hbm = pl.BlockSpec(memory_space=pl.ANY)
    left, fb, column, scale = pl.pallas_call(
        functools.partial(body, sizes),
        out_shape=(
            jax.ShapeDtypeStruct((mr, RANK), F32),
            jax.ShapeDtypeStruct((dn * zn, cz, RANK), F32),
            jax.ShapeDtypeStruct((1, RANK), F32),
            jax.ShapeDtypeStruct((1, RANK), F32),
        ),
        in_specs=[pl.BlockSpec(memory_space=pltpu.HBM)] * 2,
        out_specs=(whole,) * 4,
        scratch_shapes=[
            vmem((mc, RANK), jnp.bfloat16),
            vmem((wr, mc), F32),
            vmem((mr, width), F32),
            vmem((3, width, mr), jnp.bfloat16),
            vmem((wr, RANK), F32),
            vmem((tn, br, RANK), F32),
            vmem((mr, RANK), F32),
            vmem((RANK, RANK), F32),
            vmem((fn, RANK // fn, RANK), F32),
            vmem((RANK, RANK), F32),
            vmem((RANK, RANK), F32),
            vmem((RANK, RANK), F32),
            vmem((width, RANK), F32),
            vmem((2, fn, most, RANK), F32),
            vmem((dn * zn, cz, RANK), F32),
            vmem((8, RANK), F32),
            vmem((fn, 8, RANK), F32),
            vmem((8, RANK), F32),
            vmem((tn, 8, RANK), F32),
            pltpu.SemaphoreType.DMA((15,)),
            pltpu.SemaphoreType.DMA((14,)),
            pltpu.SemaphoreType.DMA((14,)),
        ],
        compiler_params=pltpu.CompilerParams(
            collective_id=0, has_side_effects=True, vmem_limit_bytes=LIMIT
        ),
    )(pltpu.with_memory_space_constraint(momentum, pltpu.HBM), pltpu.with_memory_space_constraint(previous, pltpu.HBM))
    parts = 4 if dn * zn % 4 == 0 and dn * zn * cz // 4 % 16 == 0 else 1
    left, right, column = pl.pallas_call(
        write_out,
        out_shape=(
            jax.ShapeDtypeStruct((mr, RANK), F32),
            jax.ShapeDtypeStruct((mc, RANK), jnp.bfloat16),
            jax.ShapeDtypeStruct((1, RANK), F32),
        ),
        in_specs=[whole] * 4,
        out_specs=(hbm,) * 3,
        scratch_shapes=[
            vmem((parts, mc // parts, RANK), jnp.bfloat16),
            pltpu.SemaphoreType.DMA((parts + 2,)),
        ],
        compiler_params=pltpu.CompilerParams(vmem_limit_bytes=16 * 2**20),
    )(fb, left, column, scale)
    return left, right, column.reshape(RANK)


def solution(mesh):
    dn, fn, tn = (mesh.shape[name] for name in ("dp", "fsdp", "tensor"))

    def run(momentum, previous):
        sizes = (dn, fn, tn, momentum.shape[0], momentum.shape[1])
        return jax.shard_map(
            functools.partial(shards, sizes),
            mesh=mesh,
            in_specs=(P("fsdp", "tensor"), P("tensor", None)),
            out_specs=(P("fsdp", None), P("tensor", None), P()),
            check_vma=False,
        )(momentum, previous)

    return run
```
